32 devices in a mesh: view: 4 (over y, core), wide: 8 (over z, x).
Axes of the slice: x: 2, y: 2, z: 4, core: 2. Of those that a mesh axis runs over, the one named last changes fastest.
Arguments:
- splats: float32 [7, 262144], P(None, 'wide'), may hold values from -3 to 1024, as said below
- camera: float32 [4, 6], P('view'), may hold values from -2 to 2, as said below
- column_perm: int32 [4, 8, 32], P('view', None, 'wide'), may hold values from 0 to 31, as said below
- block_lists: int32 [4, 8, 32, 4], P('view', None, 'wide'), may hold values from 0 to 2047, as said below
- list_lengths: int32 [4, 8, 32], P('view', None, 'wide'), may hold values from 1 to 4, 64 in all within a row
- target: float32 [4, 3, 256, 1024], P('view', None, 'wide'), may hold values from 0.1 to 1
Outputs:
- rendered: float32 [4, 3, 256, 1024], P('view', None, 'wide')
- splat_grads: float32 [7, 262144], P(None, 'wide')
The draws below stay inside these ranges and needn't reach their ends.
Inputs may be any that keep to these rules, and one draw needn't show every extreme that they name: `column_perm`: each [v, r, :] is a permutation of 0 .. 31. `block_lists`: entry [v, r, s, k] = h * 256 + r * 32 + column_perm[v, r, s] for a holder h in 0 .. 7; the holders of one tile's list differ; the list entries held by one device name each holder exactly 16 times. `splats`: splat j belongs to block j // 128; its centre lies inside tile t = (j // 128) % 256 of the screen, t = 32 row + column. Log-scales lie in [log 0.7, log 2], opacity logits in [-3, 2], colours in [0, 1]. `camera`: A00 and A11 lie in [0.998, 1.002], A01 and A10 in [-0.002, 0.002], b0 and b1 in [-2, 2].
All inputs are finite; a program needn't handle non-finite values. No bound on the sum of `list_lengths` on one device may be relied on, other than what follows from the above.
Results may differ from the reference program's by a relative error of at most 0.0045.
Values may be sent and summed in bfloat16 or wider, within the bound.
A program may use at most 64 MiB of HBM per device.

```python
import math
import jax
import jax.numpy as jnp
import numpy as np
from jax import lax

TILE = 32
BLOCK = 128
LMAX = 4
HALF = 5
TILE_COLS = 32
ROWS = 8
VIEWS = 4
HEIGHT = 256
WIDTH = 1024
TILES = 256
BLK_DEV = 256
SPLATS = 262144
N_WIDE = 8


def shared_columns(key):
    key_list = jax.random.split(key, VIEWS * ROWS)
    columns = jax.vmap(lambda single: jax.random.permutation(single, TILE_COLS))(key_list)
    return columns.reshape(VIEWS, ROWS, TILE_COLS).astype(jnp.int32)


def draw_column_perm(key, part):
    columns = shared_columns(key)
    return columns


def draw_block_lists(key, part):
    columns = shared_columns(key)
    key = jax.random.fold_in(key, 5)
    key_start, key_depth, key_label = jax.random.split(key, 3)
    per_row = TILE_COLS // N_WIDE
    residues = jnp.arange(TILE_COLS, dtype=jnp.int32) % N_WIDE
    start_keys = jax.random.split(key_start, VIEWS * N_WIDE)
    starts = jax.vmap(lambda single: jax.random.permutation(single, residues))(start_keys)
    starts = starts.reshape(VIEWS, N_WIDE, ROWS, per_row).transpose(0, 2, 1, 3).reshape(VIEWS, ROWS, TILE_COLS)
    depth_keys = jax.random.split(key_depth, VIEWS * ROWS * TILE_COLS)
    depth_order = jax.vmap(lambda single: jax.random.permutation(single, LMAX))(depth_keys)
    depth_order = depth_order.reshape(VIEWS, ROWS, TILE_COLS, LMAX).astype(jnp.int32)
    label_keys = jax.random.split(key_label, VIEWS * N_WIDE)
    label_values = jax.vmap(lambda single: jax.random.permutation(single, N_WIDE))(label_keys)
    label_values = jnp.repeat(label_values.reshape(VIEWS, N_WIDE, N_WIDE).astype(jnp.int32), per_row, axis=1)
    window = (starts[..., None] + depth_order) % N_WIDE
    holders = jnp.take_along_axis(jnp.broadcast_to(label_values[:, None], (VIEWS, ROWS, TILE_COLS, N_WIDE)), window, axis=3)
    tile_ids = jnp.arange(ROWS, dtype=jnp.int32)[None, :, None] * TILE_COLS + columns
    return (holders * BLK_DEV + tile_ids[..., None]).astype(jnp.int32)


def draw_splats(key, part):
    key = jax.random.fold_in(key, 9)
    key_list = jax.random.split(key, 7)
    splat_ids = jnp.arange(SPLATS, dtype=jnp.int32)
    home_tile = splat_ids // BLOCK % BLK_DEV
    tile_row = (home_tile // TILE_COLS).astype(jnp.float32)
    tile_col = (home_tile % TILE_COLS).astype(jnp.float32)
    uniforms = [jax.random.uniform(key_list[index], (SPLATS,), jnp.float32) for index in range(7)]
    shaped = uniforms
    low_scale = jnp.log(0.7)
    high_scale = jnp.log(2.0)
    centre_x = TILE * tile_col + TILE * (0.15 + 0.7 * shaped[0])
    centre_y = TILE * tile_row + TILE * (0.15 + 0.7 * shaped[1])
    log_scale = low_scale + (high_scale - low_scale) * shaped[2]
    logit = -3.0 + 5.0 * shaped[3]
    return jnp.stack([centre_x, centre_y, log_scale, logit, shaped[4], shaped[5], shaped[6]]).astype(jnp.float32)


def draw_camera(key, part):
    key = jax.random.fold_in(key, 13)
    unit = jax.random.uniform(key, (VIEWS, 6), jnp.float32, -1.0, 1.0)
    spread = jnp.array([0.002, 0.002, 0.002, 0.002, TILE / 16.0, TILE / 16.0], jnp.float32)
    centre = jnp.array([1.0, 0.0, 0.0, 1.0, 0.0, 0.0], jnp.float32)
    return (centre + spread * unit).astype(jnp.float32)


def levels(rng, shape, pieces, least, largest):
    gain, own = 1.0, jax.random.fold_in(rng, 6)
    for dim, parts in pieces:
        steps = jnp.exp(jax.random.uniform(jax.random.fold_in(own, dim), (parts,), jnp.float32, least / len(pieces), largest / len(pieces)))
        gain = gain * jnp.repeat(steps, shape[dim] // parts).reshape([-1 if axis == dim else 1 for axis in range(len(shape))])
    return gain


def length_profile(amount, total, reach, skew):
    weights = [(1 << 20) // math.isqrt(rank ** skew) + 1 for rank in range(2, amount + 1)]
    surplus, holding = total - reach - (amount - 1), [1] * (amount - 1)
    while surplus > 0:
        free = [i for i in range(amount - 1) if holding[i] < reach]
        mass, remaining = sum([weights[i] for i in free]), surplus
        for i in free:
            more = min(reach - holding[i], max(1, remaining * weights[i] // mass), surplus)
            holding[i] = holding[i] + more
            surplus = surplus - more
    return np.array([reach] + holding)


def uneven_parts(stream_key, amount, total, bound, lean):
    if amount == 2:
        one = jax.random.randint(stream_key, (), max(1, total - bound), min(bound, total - 1) + 1)
        return jnp.stack([one, total - one])
    sizes = jnp.asarray(length_profile(amount, total, bound, lean), jnp.int32)
    pairs = (amount - 1) // 2
    giver, receiver = sizes[1:1 + 2 * pairs:2], sizes[2:2 + 2 * pairs:2]
    slack = jnp.minimum(giver - 1, bound - receiver)
    shifted = jax.random.randint(jax.random.fold_in(stream_key, 1), (pairs,), 0, 1 << 20) % (slack + 1)
    sizes = sizes.at[1:1 + 2 * pairs:2].set(giver - shifted).at[2:2 + 2 * pairs:2].set(receiver + shifted)
    return sizes[jax.random.permutation(jax.random.fold_in(stream_key, 2), amount)]


def setup_inputs(seed: int = 0) -> dict:
    streams_of = jax.random.split(jax.random.key(seed), 7)
    return {
        "splats": draw_splats(jax.random.fold_in(streams_of[6], 71), 0),
        "camera": draw_camera(jax.random.fold_in(streams_of[6], 71), 0),
        "column_perm": draw_column_perm(jax.random.fold_in(streams_of[6], 71), 0),
        "block_lists": draw_block_lists(jax.random.fold_in(streams_of[6], 71), 0),
        "list_lengths": jax.vmap(lambda own: uneven_parts(own, TILE_COLS, TILE_COLS * LMAX // 2, LMAX, 2))(jax.random.split(streams_of[4], VIEWS * ROWS)).reshape((VIEWS, ROWS, TILE_COLS)).astype(jnp.int32),
        "target": jnp.clip(0.1 + 0.9 * jax.random.uniform(streams_of[5], (VIEWS, 3, HEIGHT, WIDTH), jnp.float32) ** levels(streams_of[5], (VIEWS, 3, HEIGHT, WIDTH), ((0, 4), (2, 8)), -0.2, 0.2), 0.1, 1.0),
    }


first_const = 0.0001
second_const = 0.0009
blur_sigma = 1.5

def project(raw_params, camera_matrix_row):
    pos_x = raw_params[..., 0, :]
    pos_y = raw_params[..., 1, :]
    screen_x = camera_matrix_row[0] * pos_x + camera_matrix_row[1] * pos_y + camera_matrix_row[4]
    screen_y = camera_matrix_row[2] * pos_x + camera_matrix_row[3] * pos_y + camera_matrix_row[5]
    precision_term = jnp.exp(-2.0 * raw_params[..., 2, :])
    opacity = jax.nn.sigmoid(raw_params[..., 3, :])
    return jnp.stack([screen_x, screen_y, precision_term, opacity, raw_params[..., 4, :], raw_params[..., 5, :], raw_params[..., 6, :]], axis=-2)

def conic_of(camera_matrix_row):
    first = camera_matrix_row[0] * camera_matrix_row[0] + camera_matrix_row[1] * camera_matrix_row[1]
    mixed = camera_matrix_row[0] * camera_matrix_row[2] + camera_matrix_row[1] * camera_matrix_row[3]
    second = camera_matrix_row[2] * camera_matrix_row[2] + camera_matrix_row[3] * camera_matrix_row[3]
    determinant = first * second - mixed * mixed
    return (second / determinant, -mixed / determinant, first / determinant)

def block_terms(splat_block_entry, pixel_x, pixel_y, conic_form):
    delta_x = pixel_x[:, None, :] - splat_block_entry[:, 0, :, None]
    delta_y = pixel_y[:, None, :] - splat_block_entry[:, 1, :, None]
    quad_form = conic_form[0] * delta_x * delta_x + 2.0 * conic_form[1] * delta_x * delta_y + conic_form[2] * delta_y * delta_y
    return splat_block_entry[:, 3, :, None] * jnp.exp(-0.5 * splat_block_entry[:, 2, :, None] * quad_form)

def absorb(carried, splat_block_entry, coverage):
    log_trans, blended_color_sum = carried
    log_keep = jnp.log1p(-coverage)
    before = jnp.cumsum(log_keep, axis=1) - log_keep
    blend_weights = coverage * jnp.exp(log_trans[:, None, :] + before)
    blended_color_sum = blended_color_sum + jnp.einsum('ztx,zxm->ztm', splat_block_entry[:, 4:7, :], blend_weights, precision=lax.Precision.HIGHEST)
    return (log_trans + lax.optimization_barrier(jnp.sum(log_keep, axis=1)), blended_color_sum)

def composite_many(blocks, lengths, anchor_x, anchor_y, conic_form, skip_dead):
    pixel_ids = jnp.arange(TILE * TILE)
    pixel_x = anchor_x[:, None] + (pixel_ids % TILE).astype(jnp.float32)[None, :] + 0.5
    pixel_y = anchor_y[:, None] + (pixel_ids // TILE).astype(jnp.float32)[None, :] + 0.5
    tile_count = blocks.shape[0]
    carried = (jnp.zeros((tile_count, TILE * TILE), jnp.float32), jnp.zeros((tile_count, 3, TILE * TILE), jnp.float32))
    for layer_step in range(blocks.shape[1]):
        splat_block_entry = blocks[:, layer_step]
        live_rows = (lengths > layer_step)[:, None, None]

        def apply_block(carried, splat_block_entry=splat_block_entry, live_rows=live_rows):
            coverage = jnp.where(live_rows, block_terms(splat_block_entry, pixel_x, pixel_y, conic_form), 0.0)
            return absorb(carried, splat_block_entry, coverage)
        apply_block = jax.checkpoint(apply_block)
        if skip_dead:
            carried = lax.cond(jnp.max(lengths) > layer_step, apply_block, lambda unchanged: unchanged, carried)
        else:
            carried = apply_block(carried)
    return carried[1]

def blur_taps():
    raw_taps = [math.exp(-(offset - HALF) ** 2 / (2.0 * blur_sigma ** 2)) for offset in range(2 * HALF + 1)]
    tap_total = sum(raw_taps)
    return [kernel_tap_value / tap_total for kernel_tap_value in raw_taps]

def blur_field(field, out_rows):
    tap_list = blur_taps()
    field_width = field.shape[2]
    padded_input = jnp.pad(field, ((0, 0), (0, 0), (HALF, HALF)))
    across = tap_list[0] * padded_input[:, :, 0:field_width]
    for offset in range(1, 2 * HALF + 1):
        across = across + tap_list[offset] * padded_input[:, :, offset:offset + field_width]
    result = tap_list[0] * across[:, 0:out_rows]
    for offset in range(1, 2 * HALF + 1):
        result = result + tap_list[offset] * across[:, offset:offset + out_rows]
    return result

def structure_loss(image_rows, target_rows, out_rows, row_weight, loss_scale):
    mean_image = blur_field(image_rows, out_rows)
    mean_target = blur_field(target_rows, out_rows)
    spread_image = blur_field(image_rows * image_rows, out_rows) - mean_image * mean_image
    spread_target = blur_field(target_rows * target_rows, out_rows) - mean_target * mean_target
    joint_spread = blur_field(image_rows * target_rows, out_rows) - mean_image * mean_target
    numerator = (2.0 * mean_image * mean_target + first_const) * (2.0 * joint_spread + second_const)
    denominator = (mean_image * mean_image + mean_target * mean_target + first_const) * (spread_image + spread_target + second_const)
    return jnp.sum(row_weight[None, :, None] * (1.0 - numerator / denominator)) / loss_scale

def render_view(raw_params, camera_matrix_row, columns, lists, lengths):
    projected = project(raw_params, camera_matrix_row)
    by_block = projected.reshape(7, SPLATS // BLOCK, BLOCK).transpose(1, 0, 2)
    conic_form = conic_of(camera_matrix_row)
    gathered = by_block[lists.reshape(TILES, LMAX).astype(jnp.int32)]
    tile_rows = jnp.repeat(jnp.arange(ROWS, dtype=jnp.int32), TILE_COLS)
    tile_cols = columns.reshape(TILES).astype(jnp.int32)
    group_total = TILES // 16

    def draw_group(bundle):
        blocks, group_lengths, group_rows, group_cols = bundle
        return composite_many(blocks, group_lengths, (group_cols * TILE).astype(jnp.float32), (group_rows * TILE).astype(jnp.float32), conic_form, False)
    colors = lax.map(draw_group, (gathered.reshape(group_total, 16, LMAX, 7, BLOCK), lengths.reshape(group_total, 16), tile_rows.reshape(group_total, 16), tile_cols.reshape(group_total, 16)))
    colors = colors.reshape(TILES, 3, TILE * TILE)
    grid = jnp.zeros((ROWS, TILE_COLS, 3, TILE * TILE), jnp.float32).at[tile_rows, tile_cols].set(colors)
    return grid.reshape(ROWS, TILE_COLS, 3, TILE, TILE).transpose(2, 0, 3, 1, 4).reshape(3, HEIGHT, WIDTH)

def reference(splats, camera, column_perm, block_lists, list_lengths, target):
    row_weight = jnp.ones((HEIGHT,), jnp.float32)
    images = []
    grad_total = jnp.zeros((7, SPLATS), jnp.float32)
    for view_index in range(VIEWS):

        def view_loss(raw_params):
            view_image = render_view(raw_params, camera[view_index], column_perm[view_index], block_lists[view_index], list_lengths[view_index])
            image_rows = jnp.pad(view_image, ((0, 0), (HALF, HALF), (0, 0)))
            target_rows = jnp.pad(target[view_index], ((0, 0), (HALF, HALF), (0, 0)))
            return (structure_loss(image_rows, target_rows, HEIGHT, row_weight, 3.0 * VIEWS), view_image)
        (loss_value, view_image), grad_view = jax.value_and_grad(view_loss, has_aux=True)(splats)
        rounded = lax.optimization_barrier(grad_view.astype(jnp.bfloat16))
        grad_total = grad_total + rounded.astype(jnp.float32)
        images.append(view_image)
    return (jnp.stack(images), grad_total)
```

```python
import functools
import math

import jax
import jax.numpy as jnp
from jax import lax
from jax.experimental import pallas as pl
from jax.experimental.pallas import tpu as pltpu
from jax.sharding import PartitionSpec as P

TILE = 32
BLOCK = 128
HALF = 5


first_const = 0.0001
second_const = 0.0009
blur_sigma = 1.5


def with_halo(array, sides, width):
    for axis, dim in sides:
        size, length = (lax.axis_size(axis), array.shape[dim])
        up = [(i, (i + 1) % size) for i in range(size - 1)]
        down = [(j, i) for i, j in up]
        last = lax.slice_in_dim(array, length - width, length, axis=dim)
        leading = lax.slice_in_dim(array, 0, width, axis=dim)
        before = lax.ppermute(last, axis, up)
        after = lax.ppermute(leading, axis, down)
        array = jnp.concatenate([before, array, after], axis=dim)
    return array


def project(raw_params, camera_matrix_row):
    pos_x = raw_params[..., 0, :]
    pos_y = raw_params[..., 1, :]
    screen_x = camera_matrix_row[0] * pos_x + camera_matrix_row[1] * pos_y + camera_matrix_row[4]
    screen_y = camera_matrix_row[2] * pos_x + camera_matrix_row[3] * pos_y + camera_matrix_row[5]
    precision_term = jnp.exp(-2.0 * raw_params[..., 2, :])
    opacity = jax.nn.sigmoid(raw_params[..., 3, :])
    return jnp.stack(
        [
            screen_x,
            screen_y,
            precision_term,
            opacity,
            raw_params[..., 4, :],
            raw_params[..., 5, :],
            raw_params[..., 6, :],
            jnp.zeros_like(pos_x),
        ],
        axis=-2,
    )


def conic_of(camera_matrix_row):
    first = (
        camera_matrix_row[0] * camera_matrix_row[0] + camera_matrix_row[1] * camera_matrix_row[1]
    )
    mixed = (
        camera_matrix_row[0] * camera_matrix_row[2] + camera_matrix_row[1] * camera_matrix_row[3]
    )
    second = (
        camera_matrix_row[2] * camera_matrix_row[2] + camera_matrix_row[3] * camera_matrix_row[3]
    )
    determinant = first * second - mixed * mixed
    return (second / determinant, -mixed / determinant, first / determinant)


CHUNK = 8
PIXELS = TILE * TILE
SPAN = CHUNK * TILE
LOG2E = math.log2(math.e)


def split_pair(values):
    high = values.astype(jnp.bfloat16)
    low = (values - high.astype(jnp.float32)).astype(jnp.bfloat16)
    return jnp.concatenate([high, low], axis=1)


def splat_rows(params, scalars, anchor_x, anchor_y):
    offset_x = params[0:1] - anchor_x
    offset_y = params[1:2] - anchor_y
    factor = (-0.5 * LOG2E) * params[2:3]
    across = lax.broadcasted_iota(jnp.int32, (TILE, BLOCK), 0).astype(jnp.float32) + 0.5
    delta_x = across - offset_x
    plane = (factor * scalars[0]) * delta_x * delta_x + jnp.log2(params[3:4])
    slope = (factor * (2.0 * scalars[1])) * delta_x
    bend = factor * scalars[2]
    return offset_y, delta_x, plane, slope, bend


def chunk_delta_y(offset_y, chunk):
    down = lax.broadcasted_iota(jnp.int32, (CHUNK, 1, BLOCK), 0).astype(jnp.float32)
    return down + (chunk * CHUNK + 0.5) - offset_y[None]


def chunk_coverage(delta_y, plane, slope, bend):
    exponent = plane[None] + delta_y * (slope[None] + bend[None] * delta_y)
    return jnp.exp2(exponent).reshape(SPAN, BLOCK)


def colour_halves(params):
    colours = params[4:8]
    high = colours.astype(jnp.bfloat16).astype(jnp.float32)
    return high, colours - high


def colour_rows(params):
    high, low = colour_halves(params)
    return jnp.concatenate(
        [high, low, high, jnp.zeros((4, BLOCK), jnp.float32)], axis=0
    ).astype(jnp.bfloat16)


def colour_columns(params, place):
    eight = jnp.concatenate(colour_halves(params), axis=0)
    lane_group = lax.broadcasted_iota(jnp.int32, (BLOCK, BLOCK), 0) // 8
    spread = jnp.where(lane_group == place, jnp.concatenate([eight] * (BLOCK // 8), axis=0), 0.0)
    columns = spread.T.astype(jnp.bfloat16)
    return jnp.concatenate([columns, columns], axis=0)


def draw_kernel(group, lengths, cols, rows, scalar_ref, blocks, before_mat, out, log_trans, acc):
    slot = pl.program_id(0)
    anchor_x = (cols[slot] * TILE).astype(jnp.float32)
    anchor_y = (rows[slot] * TILE).astype(jnp.float32)
    scalars = [scalar_ref[i] for i in range(3)]
    log_trans[...] = jnp.zeros_like(log_trans)
    place = lax.rem(slot, group)

    @pl.when(place == 0)
    def clear():
        acc[...] = jnp.zeros_like(acc)

    def layer(k, unused):
        params = blocks[0, k]
        offset_y, delta_x, plane, slope, bend = splat_rows(params, scalars, anchor_x, anchor_y)
        colours = colour_columns(params, place)
        for chunk in range(TILE // CHUNK):
            span = pl.ds(chunk * SPAN, SPAN)
            coverage = chunk_coverage(chunk_delta_y(offset_y, chunk), plane, slope, bend)
            sums = jnp.dot(
                split_pair(jnp.log(1.0 - coverage)),
                before_mat[...],
                preferred_element_type=jnp.float32,
            )
            weights = coverage * jnp.exp(log_trans[span] + sums[:, :BLOCK])
            log_trans[span] += sums[:, BLOCK:]
            acc[span] += jnp.dot(
                split_pair(weights), colours, preferred_element_type=jnp.float32
            )
        return unused

    lax.fori_loop(0, lengths[slot], layer, 0)

    @pl.when(place == group - 1)
    def finish():
        turned = acc[...].T[: 8 * group].reshape(group, 8, PIXELS)
        out[...] = turned[:, 0:3] + turned[:, 4:7]


def pull_kernel(
    lengths, cols, rows, scalar_ref, blocks, grads, before_mat, after_mat, out,
    carry, weight_store, ratio_store,
):
    slot = pl.program_id(0)
    length = lengths[slot]
    anchor_x = (cols[slot] * TILE).astype(jnp.float32)
    anchor_y = (rows[slot] * TILE).astype(jnp.float32)
    scalars = [scalar_ref[i] for i in range(7)]
    carry[...] = jnp.zeros_like(carry)
    out[...] = jnp.zeros_like(out)

    def layer(k, unused):
        params = blocks[0, k]
        offset_y, delta_x, plane, slope, bend = splat_rows(params, scalars, anchor_x, anchor_y)
        for chunk in range(TILE // CHUNK):
            span = pl.ds(chunk * SPAN, SPAN)
            coverage = chunk_coverage(chunk_delta_y(offset_y, chunk), plane, slope, bend)
            log_keep = jnp.log(1.0 - coverage)
            sums = jnp.dot(
                split_pair(log_keep), before_mat[...], preferred_element_type=jnp.float32
            )
            weight_store[k, span] = coverage * jnp.exp(carry[span] + sums[:, :BLOCK])
            ratio_store[k, span] = coverage * jnp.exp(-log_keep)
            carry[span] += sums[:, BLOCK:]
        return unused

    lax.fori_loop(0, length, layer, 0)
    carry[...] = jnp.zeros_like(carry)

    def back(step, unused):
        k = length - 1 - step
        params = blocks[0, k]
        offset_y, delta_x, plane, slope, bend = splat_rows(params, scalars, anchor_x, anchor_y)
        colours = colour_rows(params)
        zeros = jnp.zeros((TILE, BLOCK), jnp.float32)
        moment_0, moment_1, moment_2 = zeros, zeros, zeros
        colour_grads = jnp.zeros((16, BLOCK), jnp.float32)
        for chunk in range(TILE // CHUNK):
            span = pl.ds(chunk * SPAN, SPAN)
            delta_y = chunk_delta_y(offset_y, chunk)
            weights = weight_store[k, span]
            chunk_grads = grads[0, :, span]
            worth = lax.dot_general(
                chunk_grads,
                colours,
                (((0,), (0,)), ((), ())),
                preferred_element_type=jnp.float32,
            )
            shares = weights * worth
            sums = jnp.dot(
                split_pair(shares), after_mat[...], preferred_element_type=jnp.float32
            )
            behind = carry[span] + sums[:, :BLOCK]
            carry[span] += sums[:, BLOCK:]
            pull = (shares - behind * ratio_store[k, span]).reshape(CHUNK, TILE, BLOCK)
            tilted = pull * delta_y
            moment_0 += jnp.sum(pull, axis=0)
            moment_1 += jnp.sum(tilted, axis=0)
            moment_2 += jnp.sum(tilted * delta_y, axis=0)
            colour_grads += jnp.dot(
                chunk_grads, weights.astype(jnp.bfloat16), preferred_element_type=jnp.float32
            )
        qa, qb, qc, a00, a01, a10, a11 = scalars
        precision = params[2:3]
        leaned = delta_x * moment_0
        grad_u = precision * jnp.sum(qa * leaned + qb * moment_1, axis=0, keepdims=True)
        grad_w = precision * jnp.sum(qb * leaned + qc * moment_1, axis=0, keepdims=True)
        grad_s = precision * jnp.sum(
            delta_x * (qa * leaned + (2.0 * qb) * moment_1) + qc * moment_2, axis=0, keepdims=True
        )
        grad_o = (1.0 - params[3:4]) * jnp.sum(moment_0, axis=0, keepdims=True)
        out[0, k, 0:1] = a00 * grad_u + a10 * grad_w
        out[0, k, 1:2] = a01 * grad_u + a11 * grad_w
        out[0, k, 2:3] = grad_s
        out[0, k, 3:4] = grad_o
        out[0, k, 4:8] = colour_grads[0:4] + colour_grads[8:12]
        return unused

    lax.fori_loop(0, length, back, 0)


def triangle(after):
    row = jnp.arange(2 * BLOCK)[:, None] % BLOCK
    col = jnp.arange(2 * BLOCK)[None, :]
    inside = row > col if after else row < col
    return (inside | (col >= BLOCK)).astype(jnp.bfloat16)


def whole_spec(shape):
    return pl.BlockSpec(shape, lambda *unused: (0,) * len(shape))


def slot_spec(shape):
    return pl.BlockSpec((1,) + shape, lambda slot, *unused: (slot,) + (0,) * len(shape))


def draw_tiles(lengths, cols, rows, scalars, blocks):
    slots, depth = blocks.shape[0], blocks.shape[1]
    group = math.gcd(slots, BLOCK // 8)
    return pl.pallas_call(
        functools.partial(draw_kernel, group),
        grid_spec=pltpu.PrefetchScalarGridSpec(
            num_scalar_prefetch=4,
            grid=(slots,),
            in_specs=[slot_spec((depth, 8, BLOCK)), whole_spec((2 * BLOCK, 2 * BLOCK))],
            out_specs=pl.BlockSpec(
                (group, 3, PIXELS), lambda slot, *unused: (slot // group, 0, 0)
            ),
            scratch_shapes=[
                pltpu.VMEM((PIXELS, BLOCK), jnp.float32),
                pltpu.VMEM((PIXELS, BLOCK), jnp.float32),
            ],
        ),
        out_shape=jax.ShapeDtypeStruct((slots, 3, PIXELS), jnp.float32),
        compiler_params=pltpu.CompilerParams(vmem_limit_bytes=32 * 1024 * 1024),
    )(lengths, cols, rows, scalars, blocks, triangle(False))


def pull_tiles(lengths, cols, rows, scalars, blocks, grads):
    slots, depth = blocks.shape[0], blocks.shape[1]
    return pl.pallas_call(
        pull_kernel,
        grid_spec=pltpu.PrefetchScalarGridSpec(
            num_scalar_prefetch=4,
            grid=(slots,),
            in_specs=[
                slot_spec((depth, 8, BLOCK)),
                slot_spec((16, PIXELS)),
                whole_spec((2 * BLOCK, 2 * BLOCK)),
                whole_spec((2 * BLOCK, 2 * BLOCK)),
            ],
            out_specs=slot_spec((depth, 8, BLOCK)),
            scratch_shapes=[
                pltpu.VMEM((PIXELS, BLOCK), jnp.float32),
                pltpu.VMEM((depth, PIXELS, BLOCK), jnp.float32),
                pltpu.VMEM((depth, PIXELS, BLOCK), jnp.float32),
            ],
        ),
        out_shape=jax.ShapeDtypeStruct((slots, depth, 8, BLOCK), jnp.float32),
        compiler_params=pltpu.CompilerParams(vmem_limit_bytes=32 * 1024 * 1024),
    )(lengths, cols, rows, scalars, blocks, grads, triangle(False), triangle(True))


def blur_taps():
    raw_taps = [
        math.exp(-((offset - HALF) ** 2) / (2.0 * blur_sigma**2)) for offset in range(2 * HALF + 1)
    ]
    tap_total = sum(raw_taps)
    return [kernel_tap_value / tap_total for kernel_tap_value in raw_taps]


def blur_field(field, out_rows):
    tap_list = blur_taps()
    field_width = field.shape[2]
    padded_input = jnp.pad(field, ((0, 0), (0, 0), (HALF, HALF)))
    across = tap_list[0] * padded_input[:, :, 0:field_width]
    for offset in range(1, 2 * HALF + 1):
        across = across + tap_list[offset] * padded_input[:, :, offset : offset + field_width]
    result = tap_list[0] * across[:, 0:out_rows]
    for offset in range(1, 2 * HALF + 1):
        result = result + tap_list[offset] * across[:, offset : offset + out_rows]
    return result


def structure_loss(image_rows, target_rows, out_rows, row_weight, loss_scale):
    mean_image = blur_field(image_rows, out_rows)
    mean_target = blur_field(target_rows, out_rows)
    spread_image = blur_field(image_rows * image_rows, out_rows) - mean_image * mean_image
    spread_target = blur_field(target_rows * target_rows, out_rows) - mean_target * mean_target
    joint_spread = blur_field(image_rows * target_rows, out_rows) - mean_image * mean_target
    numerator = (2.0 * mean_image * mean_target + first_const) * (2.0 * joint_spread + second_const)
    denominator = (mean_image * mean_image + mean_target * mean_target + first_const) * (
        spread_image + spread_target + second_const
    )
    return jnp.sum(row_weight[None, :, None] * (1.0 - numerator / denominator)) / loss_scale


def add_views(partial):
    views = lax.axis_size("view")
    half = partial.shape[1] // 2
    odd = lax.rem(lax.axis_index("view"), 2) == 1
    mates = [(i, i ^ 1) for i in range(views)]
    left, right = partial[:, :half], partial[:, half:]
    theirs = lax.ppermute(jnp.where(odd, left, right), "view", mates)
    pair_sum = jnp.where(odd, right, left).astype(jnp.float32) + theirs.astype(jnp.float32)
    others = [
        lax.ppermute(pair_sum, "view", [(i, (i + 2 * step) % views) for i in range(views)])
        for step in range(1, views // 2)
    ]
    total = pair_sum
    for other in others:
        total = total + other
    mate_total = lax.ppermute(total, "view", mates)
    return jnp.concatenate(
        [jnp.where(odd, mate_total, total), jnp.where(odd, total, mate_total)], axis=1
    )


def on_device(splats, camera, column_perm, block_lists, list_lengths, target):
    wide_total = lax.axis_size("wide")
    view_total = lax.axis_size("view")
    camera_matrix_row = camera[0]
    conic_form = conic_of(camera_matrix_row)
    block_grand_total = splats.shape[1] // BLOCK
    stored = splats.reshape(7, block_grand_total, BLOCK).transpose(1, 0, 2)
    projected = project(stored, camera_matrix_row)
    row_total = column_perm.shape[1]
    per_row = column_perm.shape[2]
    slot_total = row_total * per_row
    list_depth = block_lists.shape[3]
    entries = block_lists.reshape(-1)
    entry_total = entries.shape[0]
    capacity = entry_total // wide_total
    holder = entries // block_grand_total
    local_ids = entries % block_grand_total
    owner_hits = (holder[:, None] == jnp.arange(wide_total, dtype=jnp.int32)[None, :]).astype(
        jnp.int32
    )
    bucket_rank = jnp.sum((jnp.cumsum(owner_hits, axis=0) - owner_hits) * owner_hits, axis=1)
    bucket_slot = holder * capacity + bucket_rank
    hits = (
        bucket_slot[:, None] == jnp.arange(entry_total, dtype=jnp.int32)[None, :]
    ).astype(jnp.int32)
    requests = jnp.sum(hits * local_ids[:, None], axis=0).reshape(wide_total, capacity)
    notes = lax.all_to_all(
        jnp.concatenate([requests, column_perm[0]], axis=1),
        "wide",
        split_axis=0,
        concat_axis=0,
        tiled=True,
    )
    asked, band_cols = notes[:, :capacity], notes[:, capacity:].reshape(slot_total)
    arrived = lax.all_to_all(projected[asked], "wide", split_axis=0, concat_axis=0, tiled=True)
    entry_blocks = arrived.reshape(entry_total, 8, BLOCK)[bucket_slot]
    slot_blocks = entry_blocks.reshape(slot_total, list_depth, 8, BLOCK)
    slot_lengths = list_lengths.reshape(slot_total)
    slot_rows = jnp.repeat(jnp.arange(row_total, dtype=jnp.int32), per_row)
    slot_cols = column_perm.reshape(slot_total)
    scalars = jnp.concatenate(
        [jnp.stack(conic_form), camera_matrix_row[:4], jnp.zeros((1,), jnp.float32)]
    )
    colors = draw_tiles(slot_lengths, slot_cols, slot_rows, scalars, slot_blocks)
    sending = colors.reshape(row_total, per_row, 3, TILE * TILE)
    band_tiles = lax.all_to_all(sending, "wide", split_axis=0, concat_axis=0, tiled=True)
    band_tiles = band_tiles.reshape(slot_total, 3, TILE * TILE)
    column_ids = jnp.arange(slot_total, dtype=jnp.int32)
    placement = jnp.sum(
        column_ids[:, None] * (band_cols[:, None] == column_ids[None, :]).astype(jnp.int32), axis=0
    )
    image_band = (
        band_tiles[placement]
        .reshape(slot_total, 3, TILE, TILE)
        .transpose(1, 2, 0, 3)
        .reshape(3, TILE, slot_total * TILE)
    )
    margin = HALF
    paired = jnp.stack([image_band, target[0]])
    extended = with_halo(paired, (("wide", 2),), margin)
    loss_scale = 3.0 * view_total
    row_weight = jnp.ones((TILE,), jnp.float32)
    grad_rows = jax.grad(
        lambda rows_now: structure_loss(rows_now, extended[1], TILE, row_weight, loss_scale)
    )(extended[0])
    band_grad = grad_rows[:, HALF : HALF + TILE]
    rim_rows = jnp.concatenate([grad_rows[:, :HALF], grad_rows[:, HALF + TILE :]], axis=1)
    received = with_halo(rim_rows, (("wide", 1),), HALF)
    band_grad = (
        band_grad.at[:, :HALF]
        .add(received[:, :HALF])
        .at[:, TILE - HALF :]
        .add(received[:, 3 * HALF :])
    )
    grad_tiles = (
        band_grad.reshape(3, TILE, slot_total, TILE)
        .transpose(2, 0, 1, 3)
        .reshape(slot_total, 3, TILE * TILE)
    )
    by_slot = grad_tiles[band_cols].reshape(
        wide_total, per_row, 3, TILE * TILE
    )
    color_grads = lax.all_to_all(by_slot, "wide", split_axis=0, concat_axis=0, tiled=True).reshape(
        slot_total, 3, TILE * TILE
    )
    once = jnp.pad(color_grads, ((0, 0), (0, 1), (0, 0)))
    high = lax.reduce_precision(once, 8, 7)
    doubled = jnp.concatenate([high, high, once - high, jnp.zeros_like(once)], axis=1).astype(
        jnp.bfloat16
    )
    entry_grads = pull_tiles(slot_lengths, slot_cols, slot_rows, scalars, slot_blocks, doubled)
    entry_grads = entry_grads.reshape(entry_total, 8 * BLOCK).astype(jnp.bfloat16)
    returning = jnp.dot(
        hits.T.astype(jnp.bfloat16), entry_grads, preferred_element_type=jnp.float32
    ).astype(jnp.bfloat16)
    returned = lax.all_to_all(
        returning.reshape(wide_total, capacity, 8 * BLOCK)[:, :, : 7 * BLOCK],
        "wide",
        split_axis=0,
        concat_axis=0,
        tiled=True,
    ).reshape(entry_total, 7 * BLOCK)
    held_ids = jnp.arange(block_grand_total, dtype=jnp.int32)
    held_hits = (held_ids[:, None] == asked.reshape(entry_total)[None, :]).astype(jnp.bfloat16)
    partial_rows = (
        jnp.dot(held_hits, returned, preferred_element_type=jnp.float32)
        .astype(jnp.bfloat16)
        .reshape(block_grand_total, 7, BLOCK)
    )
    splat_grads = add_views(
        partial_rows.transpose(1, 0, 2).reshape(7, block_grand_total * BLOCK)
    )
    return (image_band[None], splat_grads)


def solution(mesh):
    in_specs = (
        P(None, "wide"),
        P("view", None),
        P("view", None, "wide"),
        P("view", None, "wide", None),
        P("view", None, "wide"),
        P("view", None, "wide", None),
    )
    out_specs = (P("view", None, "wide", None), P(None, "wide"))
    return jax.shard_map(
        on_device, mesh=mesh, in_specs=in_specs, out_specs=out_specs, check_vma=False
    )
```

```python
import functools
import math

import jax
import jax.numpy as jnp
from jax import lax
from jax.experimental import pallas as pl
from jax.experimental.pallas import tpu as pltpu
from jax.sharding import PartitionSpec as P

TILE = 32
BLOCK = 128
HALF = 5


first_const = 0.0001
second_const = 0.0009
blur_sigma = 1.5


def with_halo(array, sides, width):
    for axis, dim in sides:
        size, length = (lax.axis_size(axis), array.shape[dim])
        up = [(i, (i + 1) % size) for i in range(size - 1)]
        down = [(j, i) for i, j in up]
        last = lax.slice_in_dim(array, length - width, length, axis=dim)
        leading = lax.slice_in_dim(array, 0, width, axis=dim)
        before = lax.ppermute(last, axis, up)
        after = lax.ppermute(leading, axis, down)
        array = jnp.concatenate([before, array, after], axis=dim)
    return array


def project(raw_params, camera_matrix_row):
    pos_x = raw_params[..., 0, :]
    pos_y = raw_params[..., 1, :]
    screen_x = camera_matrix_row[0] * pos_x + camera_matrix_row[1] * pos_y + camera_matrix_row[4]
    screen_y = camera_matrix_row[2] * pos_x + camera_matrix_row[3] * pos_y + camera_matrix_row[5]
    precision_term = jnp.exp(-2.0 * raw_params[..., 2, :])
    opacity = jax.nn.sigmoid(raw_params[..., 3, :])
    return jnp.stack(
        [
            screen_x,
            screen_y,
            precision_term,
            opacity,
            raw_params[..., 4, :],
            raw_params[..., 5, :],
            raw_params[..., 6, :],
            jnp.zeros_like(pos_x),
        ],
        axis=-2,
    )


def conic_of(camera_matrix_row):
    first = (
        camera_matrix_row[0] * camera_matrix_row[0] + camera_matrix_row[1] * camera_matrix_row[1]
    )
    mixed = (
        camera_matrix_row[0] * camera_matrix_row[2] + camera_matrix_row[1] * camera_matrix_row[3]
    )
    second = (
        camera_matrix_row[2] * camera_matrix_row[2] + camera_matrix_row[3] * camera_matrix_row[3]
    )
    determinant = first * second - mixed * mixed
    return (second / determinant, -mixed / determinant, first / determinant)


CHUNK = 16
PIXELS = TILE * TILE
SPAN = CHUNK * TILE
LOG2E = math.log2(math.e)


def split_pair(values):
    high = values.astype(jnp.bfloat16)
    low = (values - high.astype(jnp.float32)).astype(jnp.bfloat16)
    return jnp.concatenate([high, low], axis=1)


def splat_rows(params, scalars, anchor_x, anchor_y):
    offset_x = params[0:1] - anchor_x
    offset_y = params[1:2] - anchor_y
    factor = (-0.5 * LOG2E) * params[2:3]
    across = lax.broadcasted_iota(jnp.int32, (TILE, BLOCK), 0).astype(jnp.float32) + 0.5
    delta_x = across - offset_x
    plane = (factor * scalars[0]) * delta_x * delta_x + jnp.log2(params[3:4])
    slope = (factor * (2.0 * scalars[1])) * delta_x
    bend = factor * scalars[2]
    return offset_y, delta_x, plane, slope, bend


def chunk_delta_y(offset_y, chunk):
    down = lax.broadcasted_iota(jnp.int32, (CHUNK, 1, BLOCK), 0).astype(jnp.float32)
    return down + (chunk * CHUNK + 0.5) - offset_y[None]


def chunk_coverage(delta_y, plane, slope, bend):
    exponent = plane[None] + delta_y * (slope[None] + bend[None] * delta_y)
    return jnp.exp2(exponent).reshape(SPAN, BLOCK)


def colour_halves(params):
    colours = params[4:8]
    high = colours.astype(jnp.bfloat16).astype(jnp.float32)
    return high, colours - high


def colour_rows(params):
    high, low = colour_halves(params)
    return jnp.concatenate(
        [high, low, high, jnp.zeros((4, BLOCK), jnp.float32)], axis=0
    ).astype(jnp.bfloat16)


def colour_columns(params, place):
    eight = jnp.concatenate(colour_halves(params), axis=0)
    lane_group = lax.broadcasted_iota(jnp.int32, (BLOCK, BLOCK), 0) // 8
    spread = jnp.where(lane_group == place, jnp.concatenate([eight] * (BLOCK // 8), axis=0), 0.0)
    columns = spread.T.astype(jnp.bfloat16)
    return jnp.concatenate([columns, columns], axis=0)


def draw_kernel(group, lengths, cols, rows, scalar_ref, blocks, before_mat, out, log_trans, acc):
    slot = pl.program_id(0)
    anchor_x = (cols[slot] * TILE).astype(jnp.float32)
    anchor_y = (rows[slot] * TILE).astype(jnp.float32)
    scalars = [scalar_ref[i] for i in range(3)]
    log_trans[...] = jnp.zeros_like(log_trans)
    place = lax.rem(slot, group)

    @pl.when(place == 0)
    def clear():
        acc[...] = jnp.zeros_like(acc)

    def layer(k, unused):
        params = blocks[0, k]
        offset_y, delta_x, plane, slope, bend = splat_rows(params, scalars, anchor_x, anchor_y)
        colours = colour_columns(params, place)
        for chunk in range(TILE // CHUNK):
            span = pl.ds(chunk * SPAN, SPAN)
            coverage = chunk_coverage(chunk_delta_y(offset_y, chunk), plane, slope, bend)
            sums = jnp.dot(
                split_pair(jnp.log(1.0 - coverage)),
                before_mat[...],
                preferred_element_type=jnp.float32,
            )
            weights = coverage * jnp.exp(log_trans[span] + sums[:, :BLOCK])
            log_trans[span] += sums[:, BLOCK:]
            acc[span] += jnp.dot(
                split_pair(weights), colours, preferred_element_type=jnp.float32
            )
        return unused

    lax.fori_loop(0, lengths[slot], layer, 0)

    @pl.when(place == group - 1)
    def finish():
        turned = acc[...].T[: 8 * group].reshape(group, 8, PIXELS)
        out[...] = turned[:, 0:3] + turned[:, 4:7]


def pull_kernel(
    lengths, cols, rows, scalar_ref, blocks, grads, before_mat, after_mat, out,
    carry, weight_store, ratio_store,
):
    slot = pl.program_id(0)
    length = lengths[slot]
    anchor_x = (cols[slot] * TILE).astype(jnp.float32)
    anchor_y = (rows[slot] * TILE).astype(jnp.float32)
    scalars = [scalar_ref[i] for i in range(7)]
    carry[...] = jnp.zeros_like(carry)
    out[...] = jnp.zeros_like(out)

    def layer(k, unused):
        params = blocks[0, k]
        offset_y, delta_x, plane, slope, bend = splat_rows(params, scalars, anchor_x, anchor_y)
        for chunk in range(TILE // CHUNK):
            span = pl.ds(chunk * SPAN, SPAN)
            coverage = chunk_coverage(chunk_delta_y(offset_y, chunk), plane, slope, bend)
            log_keep = jnp.log(1.0 - coverage)
            sums = jnp.dot(
                split_pair(log_keep), before_mat[...], preferred_element_type=jnp.float32
            )
            weight_store[k, span] = coverage * jnp.exp(carry[span] + sums[:, :BLOCK])
            ratio_store[k, span] = coverage * jnp.exp(-log_keep)
            carry[span] += sums[:, BLOCK:]
        return unused

    lax.fori_loop(0, length, layer, 0)
    carry[...] = jnp.zeros_like(carry)

    def back(step, unused):
        k = length - 1 - step
        params = blocks[0, k]
        offset_y, delta_x, plane, slope, bend = splat_rows(params, scalars, anchor_x, anchor_y)
        colours = colour_rows(params)
        zeros = jnp.zeros((TILE, BLOCK), jnp.float32)
        moment_0, moment_1, moment_2 = zeros, zeros, zeros
        colour_grads = jnp.zeros((16, BLOCK), jnp.float32)
        for chunk in range(TILE // CHUNK):
            span = pl.ds(chunk * SPAN, SPAN)
            delta_y = chunk_delta_y(offset_y, chunk)
            weights = weight_store[k, span]
            chunk_grads = grads[0, :, span]
            worth = lax.dot_general(
                chunk_grads,
                colours,
                (((0,), (0,)), ((), ())),
                preferred_element_type=jnp.float32,
            )
            shares = weights * worth
            sums = jnp.dot(
                split_pair(shares), after_mat[...], preferred_element_type=jnp.float32
            )
            behind = carry[span] + sums[:, :BLOCK]
            carry[span] += sums[:, BLOCK:]
            pull = (shares - behind * ratio_store[k, span]).reshape(CHUNK, TILE, BLOCK)
            tilted = pull * delta_y
            moment_0 += jnp.sum(pull, axis=0)
            moment_1 += jnp.sum(tilted, axis=0)
            moment_2 += jnp.sum(tilted * delta_y, axis=0)
            colour_grads += jnp.dot(
                chunk_grads, weights.astype(jnp.bfloat16), preferred_element_type=jnp.float32
            )
        qa, qb, qc, a00, a01, a10, a11 = scalars
        precision = params[2:3]
        leaned = delta_x * moment_0
        grad_u = precision * jnp.sum(qa * leaned + qb * moment_1, axis=0, keepdims=True)
        grad_w = precision * jnp.sum(qb * leaned + qc * moment_1, axis=0, keepdims=True)
        grad_s = precision * jnp.sum(
            delta_x * (qa * leaned + (2.0 * qb) * moment_1) + qc * moment_2, axis=0, keepdims=True
        )
        grad_o = (1.0 - params[3:4]) * jnp.sum(moment_0, axis=0, keepdims=True)
        out[0, k, 0:1] = a00 * grad_u + a10 * grad_w
        out[0, k, 1:2] = a01 * grad_u + a11 * grad_w
        out[0, k, 2:3] = grad_s
        out[0, k, 3:4] = grad_o
        out[0, k, 4:8] = colour_grads[0:4] + colour_grads[8:12]
        return unused

    lax.fori_loop(0, length, back, 0)


def triangle(after):
    row = jnp.arange(2 * BLOCK)[:, None] % BLOCK
    col = jnp.arange(2 * BLOCK)[None, :]
    inside = row > col if after else row < col
    return (inside | (col >= BLOCK)).astype(jnp.bfloat16)


def whole_spec(shape):
    return pl.BlockSpec(shape, lambda *unused: (0,) * len(shape))


def slot_spec(shape):
    return pl.BlockSpec((1,) + shape, lambda slot, *unused: (slot,) + (0,) * len(shape))


def draw_tiles(lengths, cols, rows, scalars, blocks):
    slots, depth = blocks.shape[0], blocks.shape[1]
    group = math.gcd(slots, BLOCK // 8)
    return pl.pallas_call(
        functools.partial(draw_kernel, group),
        grid_spec=pltpu.PrefetchScalarGridSpec(
            num_scalar_prefetch=4,
            grid=(slots,),
            in_specs=[slot_spec((depth, 8, BLOCK)), whole_spec((2 * BLOCK, 2 * BLOCK))],
            out_specs=pl.BlockSpec(
                (group, 3, PIXELS), lambda slot, *unused: (slot // group, 0, 0)
            ),
            scratch_shapes=[
                pltpu.VMEM((PIXELS, BLOCK), jnp.float32),
                pltpu.VMEM((PIXELS, BLOCK), jnp.float32),
            ],
        ),
        out_shape=jax.ShapeDtypeStruct((slots, 3, PIXELS), jnp.float32),
        compiler_params=pltpu.CompilerParams(vmem_limit_bytes=32 * 1024 * 1024),
    )(lengths, cols, rows, scalars, blocks, triangle(False))


def pull_tiles(lengths, cols, rows, scalars, blocks, grads):
    slots, depth = blocks.shape[0], blocks.shape[1]
    return pl.pallas_call(
        pull_kernel,
        grid_spec=pltpu.PrefetchScalarGridSpec(
            num_scalar_prefetch=4,
            grid=(slots,),
            in_specs=[
                slot_spec((depth, 8, BLOCK)),
                slot_spec((16, PIXELS)),
                whole_spec((2 * BLOCK, 2 * BLOCK)),
                whole_spec((2 * BLOCK, 2 * BLOCK)),
            ],
            out_specs=slot_spec((depth, 8, BLOCK)),
            scratch_shapes=[
                pltpu.VMEM((PIXELS, BLOCK), jnp.float32),
                pltpu.VMEM((depth, PIXELS, BLOCK), jnp.float32),
                pltpu.VMEM((depth, PIXELS, BLOCK), jnp.float32),
            ],
        ),
        out_shape=jax.ShapeDtypeStruct((slots, depth, 8, BLOCK), jnp.float32),
        compiler_params=pltpu.CompilerParams(vmem_limit_bytes=32 * 1024 * 1024),
    )(lengths, cols, rows, scalars, blocks, grads, triangle(False), triangle(True))


def blur_taps():
    raw_taps = [
        math.exp(-((offset - HALF) ** 2) / (2.0 * blur_sigma**2)) for offset in range(2 * HALF + 1)
    ]
    tap_total = sum(raw_taps)
    return [kernel_tap_value / tap_total for kernel_tap_value in raw_taps]


def blur_field(field, out_rows):
    tap_list = blur_taps()
    field_width = field.shape[2]
    padded_input = jnp.pad(field, ((0, 0), (0, 0), (HALF, HALF)))
    across = tap_list[0] * padded_input[:, :, 0:field_width]
    for offset in range(1, 2 * HALF + 1):
        across = across + tap_list[offset] * padded_input[:, :, offset : offset + field_width]
    result = tap_list[0] * across[:, 0:out_rows]
    for offset in range(1, 2 * HALF + 1):
        result = result + tap_list[offset] * across[:, offset : offset + out_rows]
    return result


def structure_loss(image_rows, target_rows, out_rows, row_weight, loss_scale):
    mean_image = blur_field(image_rows, out_rows)
    mean_target = blur_field(target_rows, out_rows)
    spread_image = blur_field(image_rows * image_rows, out_rows) - mean_image * mean_image
    spread_target = blur_field(target_rows * target_rows, out_rows) - mean_target * mean_target
    joint_spread = blur_field(image_rows * target_rows, out_rows) - mean_image * mean_target
    numerator = (2.0 * mean_image * mean_target + first_const) * (2.0 * joint_spread + second_const)
    denominator = (mean_image * mean_image + mean_target * mean_target + first_const) * (
        spread_image + spread_target + second_const
    )
    return jnp.sum(row_weight[None, :, None] * (1.0 - numerator / denominator)) / loss_scale


def from_views(values):
    views = lax.axis_size("view")
    mates = [(i, i ^ 1) for i in range(views)]
    own_side = [values] + [
        lax.ppermute(values, "view", [(i, (i + 2 * step) % views) for i in range(views)])
        for step in range(1, views // 2)
    ]
    return own_side + [lax.ppermute(each, "view", mates) for each in own_side]


def on_device(splats, camera, column_perm, block_lists, list_lengths, target):
    wide_total = lax.axis_size("wide")
    view_total = lax.axis_size("view")
    camera_matrix_row = camera[0]
    conic_form = conic_of(camera_matrix_row)
    block_grand_total = splats.shape[1] // BLOCK
    stored = splats.reshape(7, block_grand_total, BLOCK).transpose(1, 0, 2)
    projected = project(stored, camera_matrix_row)
    row_total = column_perm.shape[1]
    per_row = column_perm.shape[2]
    slot_total = row_total * per_row
    list_depth = block_lists.shape[3]
    entries = block_lists.reshape(-1)
    entry_total = entries.shape[0]
    capacity = entry_total // wide_total
    holder = entries // block_grand_total
    local_ids = entries % block_grand_total
    owner_hits = (holder[:, None] == jnp.arange(wide_total, dtype=jnp.int32)[None, :]).astype(
        jnp.int32
    )
    bucket_rank = jnp.sum((jnp.cumsum(owner_hits, axis=0) - owner_hits) * owner_hits, axis=1)
    bucket_slot = holder * capacity + bucket_rank
    hits = (
        bucket_slot[:, None] == jnp.arange(entry_total, dtype=jnp.int32)[None, :]
    ).astype(jnp.int32)
    requests = jnp.sum(hits * local_ids[:, None], axis=0).reshape(wide_total, capacity)
    notes = lax.all_to_all(
        jnp.concatenate([requests, column_perm[0]], axis=1),
        "wide",
        split_axis=0,
        concat_axis=0,
        tiled=True,
    )
    asked, band_cols = notes[:, :capacity], notes[:, capacity:].reshape(slot_total)
    view_ids = from_views(asked.reshape(entry_total))
    arrived = lax.all_to_all(projected[asked], "wide", split_axis=0, concat_axis=0, tiled=True)
    entry_blocks = arrived.reshape(entry_total, 8, BLOCK)[bucket_slot]
    slot_blocks = entry_blocks.reshape(slot_total, list_depth, 8, BLOCK)
    slot_lengths = list_lengths.reshape(slot_total)
    slot_rows = jnp.repeat(jnp.arange(row_total, dtype=jnp.int32), per_row)
    slot_cols = column_perm.reshape(slot_total)
    scalars = jnp.concatenate(
        [jnp.stack(conic_form), camera_matrix_row[:4], jnp.zeros((1,), jnp.float32)]
    )
    colors = draw_tiles(slot_lengths, slot_cols, slot_rows, scalars, slot_blocks)
    sending = colors.reshape(row_total, per_row, 3, TILE * TILE)
    band_tiles = lax.all_to_all(sending, "wide", split_axis=0, concat_axis=0, tiled=True)
    band_tiles = band_tiles.reshape(slot_total, 3, TILE * TILE)
    column_ids = jnp.arange(slot_total, dtype=jnp.int32)
    placement = jnp.sum(
        column_ids[:, None] * (band_cols[:, None] == column_ids[None, :]).astype(jnp.int32), axis=0
    )
    image_band = (
        band_tiles[placement]
        .reshape(slot_total, 3, TILE, TILE)
        .transpose(1, 2, 0, 3)
        .reshape(3, TILE, slot_total * TILE)
    )
    margin = HALF
    paired = jnp.stack([image_band, target[0]])
    extended = with_halo(paired, (("wide", 2),), margin)
    loss_scale = 3.0 * view_total
    row_weight = jnp.ones((TILE,), jnp.float32)
    grad_rows = jax.grad(
        lambda rows_now: structure_loss(rows_now, extended[1], TILE, row_weight, loss_scale)
    )(extended[0])
    band_grad = grad_rows[:, HALF : HALF + TILE]
    rim_rows = jnp.concatenate([grad_rows[:, :HALF], grad_rows[:, HALF + TILE :]], axis=1)
    received = with_halo(rim_rows, (("wide", 1),), HALF)
    band_grad = (
        band_grad.at[:, :HALF]
        .add(received[:, :HALF])
        .at[:, TILE - HALF :]
        .add(received[:, 3 * HALF :])
    )
    grad_tiles = (
        band_grad.reshape(3, TILE, slot_total, TILE)
        .transpose(2, 0, 1, 3)
        .reshape(slot_total, 3, TILE * TILE)
    )
    by_slot = grad_tiles[band_cols].reshape(
        wide_total, per_row, 3, TILE * TILE
    )
    color_grads = lax.all_to_all(by_slot, "wide", split_axis=0, concat_axis=0, tiled=True).reshape(
        slot_total, 3, TILE * TILE
    )
    once = jnp.pad(color_grads, ((0, 0), (0, 1), (0, 0)))
    high = lax.reduce_precision(once, 8, 7)
    doubled = jnp.concatenate([high, high, once - high, jnp.zeros_like(once)], axis=1).astype(
        jnp.bfloat16
    )
    entry_grads = pull_tiles(slot_lengths, slot_cols, slot_rows, scalars, slot_blocks, doubled)
    entry_grads = entry_grads.reshape(entry_total, 8 * BLOCK).astype(jnp.bfloat16)
    returning = jnp.dot(
        hits.T.astype(jnp.bfloat16), entry_grads, preferred_element_type=jnp.float32
    ).astype(jnp.bfloat16)
    returned = lax.all_to_all(
        returning.reshape(wide_total, capacity, 8 * BLOCK)[:, :, : 7 * BLOCK],
        "wide",
        split_axis=0,
        concat_axis=0,
        tiled=True,
    ).reshape(entry_total, 7 * BLOCK)
    held_ids = jnp.arange(block_grand_total, dtype=jnp.int32)
    all_ids = jnp.concatenate(view_ids, axis=0)
    held_hits = (held_ids[:, None] == all_ids[None, :]).astype(jnp.bfloat16)
    all_rows = jnp.concatenate(from_views(returned), axis=0)
    splat_grads = (
        jnp.dot(held_hits, all_rows, preferred_element_type=jnp.float32)
        .reshape(block_grand_total, 7, BLOCK)
        .transpose(1, 0, 2)
        .reshape(7, block_grand_total * BLOCK)
    )
    return (image_band[None], splat_grads)


def solution(mesh):
    in_specs = (
        P(None, "wide"),
        P("view", None),
        P("view", None, "wide"),
        P("view", None, "wide", None),
        P("view", None, "wide"),
        P("view", None, "wide", None),
    )
    out_specs = (P("view", None, "wide", None), P(None, "wide"))
    return jax.shard_map(
        on_device, mesh=mesh, in_specs=in_specs, out_specs=out_specs, check_vma=False
    )
```

```python
import functools
import math

import jax
import jax.numpy as jnp
from jax import lax
from jax.experimental import pallas as pl
from jax.experimental.pallas import tpu as pltpu
from jax.sharding import PartitionSpec as P

TILE = 32
BLOCK = 128
HALF = 5


first_const = 0.0001
second_const = 0.0009
blur_sigma = 1.5


def with_halo(array, sides, width):
    for axis, dim in sides:
        size, length = (lax.axis_size(axis), array.shape[dim])
        up = [(i, (i + 1) % size) for i in range(size - 1)]
        down = [(j, i) for i, j in up]
        last = lax.slice_in_dim(array, length - width, length, axis=dim)
        leading = lax.slice_in_dim(array, 0, width, axis=dim)
        before = lax.ppermute(last, axis, up)
        after = lax.ppermute(leading, axis, down)
        array = jnp.concatenate([before, array, after], axis=dim)
    return array


def project(raw_params, camera_matrix_row):
    pos_x = raw_params[..., 0, :]
    pos_y = raw_params[..., 1, :]
    screen_x = camera_matrix_row[0] * pos_x + camera_matrix_row[1] * pos_y + camera_matrix_row[4]
    screen_y = camera_matrix_row[2] * pos_x + camera_matrix_row[3] * pos_y + camera_matrix_row[5]
    precision_term = jnp.exp(-2.0 * raw_params[..., 2, :])
    opacity = jax.nn.sigmoid(raw_params[..., 3, :])
    return jnp.stack(
        [
            screen_x,
            screen_y,
            precision_term,
            opacity,
            raw_params[..., 4, :],
            raw_params[..., 5, :],
            raw_params[..., 6, :],
            jnp.zeros_like(pos_x),
        ],
        axis=-2,
    )


def conic_of(camera_matrix_row):
    first = (
        camera_matrix_row[0] * camera_matrix_row[0] + camera_matrix_row[1] * camera_matrix_row[1]
    )
    mixed = (
        camera_matrix_row[0] * camera_matrix_row[2] + camera_matrix_row[1] * camera_matrix_row[3]
    )
    second = (
        camera_matrix_row[2] * camera_matrix_row[2] + camera_matrix_row[3] * camera_matrix_row[3]
    )
    determinant = first * second - mixed * mixed
    return (second / determinant, -mixed / determinant, first / determinant)


CHUNK = 16
PIXELS = TILE * TILE
SPAN = CHUNK * TILE
LOG2E = math.log2(math.e)


def split_pair(values):
    high = values.astype(jnp.bfloat16)
    low = (values - high.astype(jnp.float32)).astype(jnp.bfloat16)
    return jnp.concatenate([high, low], axis=1)


def splat_rows(params, scalars, anchor_x, anchor_y):
    offset_x = params[0:1] - anchor_x
    offset_y = params[1:2] - anchor_y
    factor = (-0.5 * LOG2E) * params[2:3]
    across = lax.broadcasted_iota(jnp.int32, (TILE, BLOCK), 0).astype(jnp.float32) + 0.5
    delta_x = across - offset_x
    plane = (factor * scalars[0]) * delta_x * delta_x + jnp.log2(params[3:4])
    slope = (factor * (2.0 * scalars[1])) * delta_x
    bend = factor * scalars[2]
    return offset_y, delta_x, plane, slope, bend


def chunk_delta_y(offset_y, chunk):
    down = lax.broadcasted_iota(jnp.int32, (CHUNK, 1, BLOCK), 0).astype(jnp.float32)
    return down + (chunk * CHUNK + 0.5) - offset_y[None]


def chunk_coverage(delta_y, plane, slope, bend):
    exponent = plane[None] + delta_y * (slope[None] + bend[None] * delta_y)
    return jnp.exp2(exponent).reshape(SPAN, BLOCK)


def colour_halves(params):
    colours = params[4:8]
    high = colours.astype(jnp.bfloat16).astype(jnp.float32)
    return high, colours - high


def colour_rows(params):
    high, low = colour_halves(params)
    return jnp.concatenate(
        [high, low, high, jnp.zeros((4, BLOCK), jnp.float32)], axis=0
    ).astype(jnp.bfloat16)


def colour_columns(params, place):
    eight = jnp.concatenate(colour_halves(params), axis=0)
    lane_group = lax.broadcasted_iota(jnp.int32, (BLOCK, BLOCK), 0) // 8
    spread = jnp.where(lane_group == place, jnp.concatenate([eight] * (BLOCK // 8), axis=0), 0.0)
    columns = spread.T.astype(jnp.bfloat16)
    return jnp.concatenate([columns, columns], axis=0)


def draw_kernel(group, lengths, cols, rows, scalar_ref, blocks, before_mat, out, log_trans, acc):
    slot = pl.program_id(0)
    anchor_x = (cols[slot] * TILE).astype(jnp.float32)
    anchor_y = (rows[slot] * TILE).astype(jnp.float32)
    scalars = [scalar_ref[i] for i in range(3)]
    log_trans[...] = jnp.zeros_like(log_trans)
    place = lax.rem(slot, group)

    @pl.when(place == 0)
    def clear():
        acc[...] = jnp.zeros_like(acc)

    def layer(k, unused):
        params = blocks[0, k]
        offset_y, delta_x, plane, slope, bend = splat_rows(params, scalars, anchor_x, anchor_y)
        colours = colour_columns(params, place)
        for chunk in range(TILE // CHUNK):
            span = pl.ds(chunk * SPAN, SPAN)
            coverage = chunk_coverage(chunk_delta_y(offset_y, chunk), plane, slope, bend)
            sums = jnp.dot(
                split_pair(jnp.log(1.0 - coverage)),
                before_mat[...],
                preferred_element_type=jnp.float32,
            )
            weights = coverage * jnp.exp(log_trans[span] + sums[:, :BLOCK])
            log_trans[span] += sums[:, BLOCK:]
            acc[span] += jnp.dot(
                split_pair(weights), colours, preferred_element_type=jnp.float32
            )
        return unused

    lax.fori_loop(0, lengths[slot], layer, 0)

    @pl.when(place == group - 1)
    def finish():
        turned = acc[...].T[: 8 * group].reshape(group, 8, PIXELS)
        out[...] = turned[:, 0:3] + turned[:, 4:7]


def pull_kernel(
    lengths, cols, rows, scalar_ref, blocks, grads, before_mat, after_mat, out,
    carry, weight_store, ratio_store,
):
    slot = pl.program_id(0)
    length = lengths[slot]
    anchor_x = (cols[slot] * TILE).astype(jnp.float32)
    anchor_y = (rows[slot] * TILE).astype(jnp.float32)
    scalars = [scalar_ref[i] for i in range(7)]
    carry[...] = jnp.zeros_like(carry)
    out[...] = jnp.zeros_like(out)

    def layer(k, unused):
        params = blocks[0, k]
        offset_y, delta_x, plane, slope, bend = splat_rows(params, scalars, anchor_x, anchor_y)
        for chunk in range(TILE // CHUNK):
            span = pl.ds(chunk * SPAN, SPAN)
            coverage = chunk_coverage(chunk_delta_y(offset_y, chunk), plane, slope, bend)
            log_keep = jnp.log(1.0 - coverage)
            sums = jnp.dot(
                split_pair(log_keep), before_mat[...], preferred_element_type=jnp.float32
            )
            weight_store[k, span] = coverage * jnp.exp(carry[span] + sums[:, :BLOCK])
            ratio_store[k, span] = coverage * jnp.exp(-log_keep)
            carry[span] += sums[:, BLOCK:]
        return unused

    lax.fori_loop(0, length, layer, 0)
    carry[...] = jnp.zeros_like(carry)

    def back(step, unused):
        k = length - 1 - step
        params = blocks[0, k]
        offset_y, delta_x, plane, slope, bend = splat_rows(params, scalars, anchor_x, anchor_y)
        colours = colour_rows(params)
        zeros = jnp.zeros((TILE, BLOCK), jnp.float32)
        moment_0, moment_1, moment_2 = zeros, zeros, zeros
        colour_grads = jnp.zeros((16, BLOCK), jnp.float32)
        for chunk in range(TILE // CHUNK):
            span = pl.ds(chunk * SPAN, SPAN)
            delta_y = chunk_delta_y(offset_y, chunk)
            weights = weight_store[k, span]
            chunk_grads = grads[0, :, span]
            worth = lax.dot_general(
                chunk_grads,
                colours,
                (((0,), (0,)), ((), ())),
                preferred_element_type=jnp.float32,
            )
            shares = weights * worth
            sums = jnp.dot(
                split_pair(shares), after_mat[...], preferred_element_type=jnp.float32
            )
            behind = carry[span] + sums[:, :BLOCK]
            carry[span] += sums[:, BLOCK:]
            pull = (shares - behind * ratio_store[k, span]).reshape(CHUNK, TILE, BLOCK)
            tilted = pull * delta_y
            moment_0 += jnp.sum(pull, axis=0)
            moment_1 += jnp.sum(tilted, axis=0)
            moment_2 += jnp.sum(tilted * delta_y, axis=0)
            colour_grads += jnp.dot(
                chunk_grads, weights.astype(jnp.bfloat16), preferred_element_type=jnp.float32
            )
        qa, qb, qc, a00, a01, a10, a11 = scalars
        precision = params[2:3]
        leaned = delta_x * moment_0
        grad_u = precision * jnp.sum(qa * leaned + qb * moment_1, axis=0, keepdims=True)
        grad_w = precision * jnp.sum(qb * leaned + qc * moment_1, axis=0, keepdims=True)
        grad_s = precision * jnp.sum(
            delta_x * (qa * leaned + (2.0 * qb) * moment_1) + qc * moment_2, axis=0, keepdims=True
        )
        grad_o = (1.0 - params[3:4]) * jnp.sum(moment_0, axis=0, keepdims=True)
        out[0, k, 0:1] = a00 * grad_u + a10 * grad_w
        out[0, k, 1:2] = a01 * grad_u + a11 * grad_w
        out[0, k, 2:3] = grad_s
        out[0, k, 3:4] = grad_o
        out[0, k, 4:8] = colour_grads[0:4] + colour_grads[8:12]
        return unused

    lax.fori_loop(0, length, back, 0)


def triangle(after):
    row = jnp.arange(2 * BLOCK)[:, None] % BLOCK
    col = jnp.arange(2 * BLOCK)[None, :]
    inside = row > col if after else row < col
    return (inside | (col >= BLOCK)).astype(jnp.bfloat16)


def whole_spec(shape):
    return pl.BlockSpec(shape, lambda *unused: (0,) * len(shape))


def slot_spec(shape):
    return pl.BlockSpec((1,) + shape, lambda slot, *unused: (slot,) + (0,) * len(shape))


def draw_tiles(lengths, cols, rows, scalars, blocks):
    slots, depth = blocks.shape[0], blocks.shape[1]
    group = math.gcd(slots, BLOCK // 8)
    return pl.pallas_call(
        functools.partial(draw_kernel, group),
        grid_spec=pltpu.PrefetchScalarGridSpec(
            num_scalar_prefetch=4,
            grid=(slots,),
            in_specs=[slot_spec((depth, 8, BLOCK)), whole_spec((2 * BLOCK, 2 * BLOCK))],
            out_specs=pl.BlockSpec(
                (group, 3, PIXELS), lambda slot, *unused: (slot // group, 0, 0)
            ),
            scratch_shapes=[
                pltpu.VMEM((PIXELS, BLOCK), jnp.float32),
                pltpu.VMEM((PIXELS, BLOCK), jnp.float32),
            ],
        ),
        out_shape=jax.ShapeDtypeStruct((slots, 3, PIXELS), jnp.float32),
        compiler_params=pltpu.CompilerParams(vmem_limit_bytes=32 * 1024 * 1024),
    )(lengths, cols, rows, scalars, blocks, triangle(False))


def pull_tiles(lengths, cols, rows, scalars, blocks, grads):
    slots, depth = blocks.shape[0], blocks.shape[1]
    return pl.pallas_call(
        pull_kernel,
        grid_spec=pltpu.PrefetchScalarGridSpec(
            num_scalar_prefetch=4,
            grid=(slots,),
            in_specs=[
                slot_spec((depth, 8, BLOCK)),
                slot_spec((16, PIXELS)),
                whole_spec((2 * BLOCK, 2 * BLOCK)),
                whole_spec((2 * BLOCK, 2 * BLOCK)),
            ],
            out_specs=slot_spec((depth, 8, BLOCK)),
            scratch_shapes=[
                pltpu.VMEM((PIXELS, BLOCK), jnp.float32),
                pltpu.VMEM((depth, PIXELS, BLOCK), jnp.float32),
                pltpu.VMEM((depth, PIXELS, BLOCK), jnp.float32),
            ],
        ),
        out_shape=jax.ShapeDtypeStruct((slots, depth, 8, BLOCK), jnp.float32),
        compiler_params=pltpu.CompilerParams(vmem_limit_bytes=32 * 1024 * 1024),
    )(lengths, cols, rows, scalars, blocks, grads, triangle(False), triangle(True))


def blur_taps():
    raw_taps = [
        math.exp(-((offset - HALF) ** 2) / (2.0 * blur_sigma**2)) for offset in range(2 * HALF + 1)
    ]
    tap_total = sum(raw_taps)
    return [kernel_tap_value / tap_total for kernel_tap_value in raw_taps]


def blur_field(field, out_rows):
    tap_list = blur_taps()
    field_width = field.shape[2]
    padded_input = jnp.pad(field, ((0, 0), (0, 0), (HALF, HALF)))
    across = tap_list[0] * padded_input[:, :, 0:field_width]
    for offset in range(1, 2 * HALF + 1):
        across = across + tap_list[offset] * padded_input[:, :, offset : offset + field_width]
    result = tap_list[0] * across[:, 0:out_rows]
    for offset in range(1, 2 * HALF + 1):
        result = result + tap_list[offset] * across[:, offset : offset + out_rows]
    return result


def structure_loss(image_rows, target_rows, out_rows, row_weight, loss_scale):
    mean_image = blur_field(image_rows, out_rows)
    mean_target = blur_field(target_rows, out_rows)
    spread_image = blur_field(image_rows * image_rows, out_rows) - mean_image * mean_image
    spread_target = blur_field(target_rows * target_rows, out_rows) - mean_target * mean_target
    joint_spread = blur_field(image_rows * target_rows, out_rows) - mean_image * mean_target
    numerator = (2.0 * mean_image * mean_target + first_const) * (2.0 * joint_spread + second_const)
    denominator = (mean_image * mean_image + mean_target * mean_target + first_const) * (
        spread_image + spread_target + second_const
    )
    return jnp.sum(row_weight[None, :, None] * (1.0 - numerator / denominator)) / loss_scale


def from_views(values):
    views = lax.axis_size("view")
    mates = [(i, i ^ 1) for i in range(views)]
    own_side = [values] + [
        lax.ppermute(values, "view", [(i, (i + 2 * step) % views) for i in range(views)])
        for step in range(1, views // 2)
    ]
    return own_side + [lax.ppermute(each, "view", mates) for each in own_side]


def on_device(splats, camera, column_perm, block_lists, list_lengths, target):
    wide_total = lax.axis_size("wide")
    view_total = lax.axis_size("view")
    camera_matrix_row = camera[0]
    conic_form = conic_of(camera_matrix_row)
    block_grand_total = splats.shape[1] // BLOCK
    stored = splats.reshape(7, block_grand_total, BLOCK).transpose(1, 0, 2)
    projected = project(stored, camera_matrix_row)
    row_total = column_perm.shape[1]
    per_row = column_perm.shape[2]
    slot_total = row_total * per_row
    list_depth = block_lists.shape[3]
    entries = block_lists.reshape(-1)
    entry_total = entries.shape[0]
    capacity = entry_total // wide_total
    holder = entries // block_grand_total
    local_ids = entries % block_grand_total
    owner_hits = (holder[:, None] == jnp.arange(wide_total, dtype=jnp.int32)[None, :]).astype(
        jnp.int32
    )
    bucket_rank = jnp.sum((jnp.cumsum(owner_hits, axis=0) - owner_hits) * owner_hits, axis=1)
    bucket_slot = holder * capacity + bucket_rank
    hits = (
        bucket_slot[:, None] == jnp.arange(entry_total, dtype=jnp.int32)[None, :]
    ).astype(jnp.int32)
    requests = jnp.sum(hits * local_ids[:, None], axis=0).reshape(wide_total, capacity)
    notes = lax.all_to_all(
        jnp.concatenate([requests, column_perm[0]], axis=1),
        "wide",
        split_axis=0,
        concat_axis=0,
        tiled=True,
    )
    asked, band_cols = notes[:, :capacity], notes[:, capacity:].reshape(slot_total)
    view_ids = from_views(asked.reshape(entry_total))
    arrived = lax.all_to_all(projected[asked], "wide", split_axis=0, concat_axis=0, tiled=True)
    entry_blocks = arrived.reshape(entry_total, 8, BLOCK)[bucket_slot]
    slot_blocks = entry_blocks.reshape(slot_total, list_depth, 8, BLOCK)
    slot_lengths = list_lengths.reshape(slot_total)
    slot_rows = jnp.repeat(jnp.arange(row_total, dtype=jnp.int32), per_row)
    slot_cols = column_perm.reshape(slot_total)
    scalars = jnp.concatenate(
        [jnp.stack(conic_form), camera_matrix_row[:4], jnp.zeros((1,), jnp.float32)]
    )
    colors = draw_tiles(slot_lengths, slot_cols, slot_rows, scalars, slot_blocks)
    sending = colors.reshape(row_total, per_row, 3, TILE * TILE)
    band_tiles = lax.all_to_all(sending, "wide", split_axis=0, concat_axis=0, tiled=True)
    band_tiles = band_tiles.reshape(slot_total, 3, TILE * TILE)
    column_ids = jnp.arange(slot_total, dtype=jnp.int32)
    placement = jnp.sum(
        column_ids[:, None] * (band_cols[:, None] == column_ids[None, :]).astype(jnp.int32), axis=0
    )
    image_band = (
        band_tiles[placement]
        .reshape(slot_total, 3, TILE, TILE)
        .transpose(1, 2, 0, 3)
        .reshape(3, TILE, slot_total * TILE)
    )
    margin = HALF
    image_rows = with_halo(image_band, (("wide", 1),), margin)
    target_rows = with_halo(target[0], (("wide", 1),), margin)
    loss_scale = 3.0 * view_total
    row_weight = jnp.ones((TILE,), jnp.float32)
    grad_rows = jax.grad(
        lambda rows_now: structure_loss(rows_now, target_rows, TILE, row_weight, loss_scale)
    )(image_rows)
    band_grad = grad_rows[:, HALF : HALF + TILE]
    rim_rows = jnp.concatenate([grad_rows[:, :HALF], grad_rows[:, HALF + TILE :]], axis=1)
    received = with_halo(rim_rows, (("wide", 1),), HALF)
    band_grad = (
        band_grad.at[:, :HALF]
        .add(received[:, :HALF])
        .at[:, TILE - HALF :]
        .add(received[:, 3 * HALF :])
    )
    grad_tiles = (
        band_grad.reshape(3, TILE, slot_total, TILE)
        .transpose(2, 0, 1, 3)
        .reshape(slot_total, 3, TILE * TILE)
    )
    by_slot = grad_tiles[band_cols].reshape(
        wide_total, per_row, 3, TILE * TILE
    )
    color_grads = lax.all_to_all(by_slot, "wide", split_axis=0, concat_axis=0, tiled=True).reshape(
        slot_total, 3, TILE * TILE
    )
    once = jnp.pad(color_grads, ((0, 0), (0, 1), (0, 0)))
    high = lax.reduce_precision(once, 8, 7)
    doubled = jnp.concatenate([high, high, once - high, jnp.zeros_like(once)], axis=1).astype(
        jnp.bfloat16
    )
    entry_grads = pull_tiles(slot_lengths, slot_cols, slot_rows, scalars, slot_blocks, doubled)
    entry_grads = entry_grads.reshape(entry_total, 8 * BLOCK).astype(jnp.bfloat16)
    returning = jnp.dot(
        hits.T.astype(jnp.bfloat16), entry_grads, preferred_element_type=jnp.float32
    ).astype(jnp.bfloat16)
    returned = lax.all_to_all(
        returning.reshape(wide_total, capacity, 8 * BLOCK)[:, :, : 7 * BLOCK],
        "wide",
        split_axis=0,
        concat_axis=0,
        tiled=True,
    ).reshape(entry_total, 7 * BLOCK)
    held_ids = jnp.arange(block_grand_total, dtype=jnp.int32)
    all_ids = jnp.concatenate(view_ids, axis=0)
    held_hits = (held_ids[:, None] == all_ids[None, :]).astype(jnp.bfloat16)
    all_rows = jnp.concatenate(from_views(returned), axis=0)
    splat_grads = (
        jnp.dot(held_hits, all_rows, preferred_element_type=jnp.float32)
        .reshape(block_grand_total, 7, BLOCK)
        .transpose(1, 0, 2)
        .reshape(7, block_grand_total * BLOCK)
    )
    return (image_band[None], splat_grads)


def solution(mesh):
    in_specs = (
        P(None, "wide"),
        P("view", None),
        P("view", None, "wide"),
        P("view", None, "wide", None),
        P("view", None, "wide"),
        P("view", None, "wide", None),
    )
    out_specs = (P("view", None, "wide", None), P(None, "wide"))
    return jax.shard_map(
        on_device, mesh=mesh, in_specs=in_specs, out_specs=out_specs, check_vma=False
    )
```
